32 devices in a mesh: space: 8 (over z, x), scal: 4 (over y, core).
Axes of the slice: x: 2, y: 2, z: 4, core: 2. Of those that a mesh axis runs over, the one named last changes fastest.
Arguments:
- scalars: float32 [128, 512, 256], P('scal', 'space'), may hold values from -6 to 6
- schmidt: float32 [128], P('scal'), may hold values from 1 to 1000
- velocity_history: bfloat16 [8, 2, 64, 256], P('scal', None, 'space'), may hold values from -0.796875 to 0.796875
- fine_src: int32 [512], replicated, may hold values from 0 to 62, as said below
- remap_weight: float32 [512], replicated, may hold values from 0 to 1
- snap_step: int32 [2], replicated, may hold values from 0 to 7
Outputs:
- transported: float32 [128, 512, 256], P('scal', 'space')
The draws below stay inside these ranges and needn't reach their ends.
Inputs may be any that keep to these rules, and one draw needn't show every extreme that they name: fine_src may name any coarse row of any tile, in no particular order.
All inputs are finite; a program needn't handle non-finite values.
Results may differ from the reference program's by a relative error of at most 0.0003.
Values may be sent and summed in bfloat16 or wider, within the bound.
A program may use at most 64 MiB of HBM per device.

```python
import math
import jax
import jax.numpy as jnp
from jax import lax

SC_DEV = 32
TX = 64
NZ = 256
CR_DEV = 8
STEPS = 2
NSCAL = 128
NX = 512
NCX = 64
NSNAP = 8
N_SCAL = 4


def draw_fine_src(key, part):
    tile_count = NX // TX
    tile_id = jnp.arange(tile_count, dtype=jnp.int32)
    column = jnp.arange(TX, dtype=jnp.int32)
    rows = jax.random.randint(jax.random.fold_in(key, 17), (tile_count, TX), 0, NCX - 1).astype(jnp.int32)
    within = jax.random.randint(jax.random.fold_in(key, 29), (tile_count, 3), 0, CR_DEV).astype(jnp.int32)
    far_tile = (tile_id + tile_count // 2) % tile_count
    before_tile = (tile_id + tile_count - 1) % tile_count
    after_tile = (tile_id + 1) % tile_count
    far_row = jnp.minimum(far_tile * CR_DEV + within[:, 0], NCX - 2)
    before_row = jnp.minimum(before_tile * CR_DEV + within[:, 1], NCX - 2)
    after_row = jnp.minimum(after_tile * CR_DEV + within[:, 2], NCX - 2)
    rows = jnp.where(column[None, :] == 0, far_row[:, None], rows)
    rows = jnp.where(column[None, :] == 1, before_row[:, None], rows)
    rows = jnp.where(column[None, :] == 2, after_row[:, None], rows)
    edge_first = (column[None, :] == 3) & (tile_id[:, None] == 0)
    edge_last = (column[None, :] == 3) & (tile_id[:, None] == tile_count - 1)
    rows = jnp.where(edge_first, NCX - 2, rows)
    rows = jnp.where(edge_last, 0, rows)
    return rows.reshape(NX).astype(jnp.int32)


def shard_levels(key, extent, pieces, least, largest):
    def one(dim, parts):
        heights = jax.random.uniform(jax.random.fold_in(jax.random.fold_in(key, 6), dim), (parts,), jnp.float32, least / len(pieces), largest / len(pieces))
        return jnp.repeat(jnp.exp(heights), extent[dim] // parts).reshape((-1,) + (1,) * (len(extent) - dim - 1))

    loudness = one(*pieces[0])
    for cut in pieces[1:]:
        loudness = loudness * one(*cut)
    return loudness


def gaussian(key, dims, spread, reach, cuts=(), held_as=jnp.bfloat16):
    level = shard_levels(key, dims, cuts, -0.22, 0.18) if cuts else 1.0
    drawn = jax.random.normal(key, dims, jnp.float32) * spread * level
    return jnp.minimum(jnp.maximum(drawn, -reach), reach).astype(held_as)


def setup_inputs(seed: int = 0) -> dict:
    streams_of = jax.random.split(jax.random.key(seed), 7)
    scalars = gaussian(streams_of[0], (NSCAL, NX, NZ), 1.0, 6.0, ((0, 4), (1, 8)), jnp.float32)
    schmidt = jnp.clip(jnp.exp(math.log(1000.0) - 6.9077553 * jax.random.uniform(streams_of[1], (NSCAL,), jnp.float32) ** shard_levels(streams_of[1], (NSCAL,), ((0, 4),), -0.2, 0.2)), 1.0, 1000.0)
    velocity_history = gaussian(streams_of[2], (NSNAP, 2, NCX, NZ), 0.2, 0.796875, ((0, 4), (2, 8)))
    fine_src = draw_fine_src(jax.random.fold_in(streams_of[6], 71), 0)
    remap_weight = jnp.clip(jax.random.uniform(streams_of[4], (NX,), jnp.float32, 0.0, 1.0), 0.0, 1.0)
    snap_step = jax.random.randint(streams_of[5], (STEPS,), 0, NSNAP).astype(jnp.int32)
    return dict(scalars=scalars, schmidt=schmidt, velocity_history=velocity_history, fine_src=fine_src, remap_weight=remap_weight, snap_step=snap_step)


diffusion_scale = 0.24


def advance(padded, velocity, diffusivity):
    center = padded[:, 1:-1]
    upper_row = padded[:, 2:]
    lower_row = padded[:, :-2]
    east_cell = jnp.roll(center, -1, axis=2)
    west_cell = jnp.roll(center, 1, axis=2)
    laplacian = upper_row + lower_row + east_cell + west_cell - 4.0 * center
    return (center - velocity[0] * (0.5 * (upper_row - lower_row))
            - velocity[1] * (0.5 * (east_cell - west_cell))
            + diffusivity[:, None, None] * laplacian)


def remap_snapshot(coarse, fine_src, remap_weight):
    coarse = coarse.astype(jnp.float32)
    lower_pick = coarse[:, fine_src]
    upper_pick = coarse[:, fine_src + 1]
    return lower_pick * (1.0 - remap_weight)[None, :, None] + upper_pick * remap_weight[None, :, None]


def reference(scalars, schmidt, velocity_history, fine_src, remap_weight, snap_step):
    diffusivity = diffusion_scale / schmidt
    velocities = [remap_snapshot(lax.dynamic_index_in_dim(velocity_history, snap_step[step_index], 0, keepdims=False), fine_src, remap_weight) for step_index in range(STEPS)]

    def one_group(operands):
        field, group_diff = operands
        for step_index in range(STEPS):
            padded = jnp.pad(field, ((0, 0), (1, 1), (0, 0)))
            field = advance(padded, velocities[step_index], group_diff)
        return field

    shaped = scalars.reshape(N_SCAL, SC_DEV, NX, NZ)
    result = lax.map(one_group, (shaped, diffusivity.reshape(N_SCAL, SC_DEV)))
    return result.reshape(NSCAL, NX, NZ)
```

```python
import functools

import jax
import jax.numpy as jnp
from jax import lax
from jax.experimental import pallas as pl
from jax.experimental.pallas import tpu as pltpu
from jax.sharding import PartitionSpec as P

MESH = pl.DeviceIdType.MESH
LANES = 128
GROUPS = 4


def gather_kernel(
    n_space, n_scal, snap, src, wgt, hist, field, halo, vel,
    mine, part, coarse, select, halo_send, halo_recv, part_send, part_recv,
    row_send, row_recv,
):
    tile = lax.axis_index("space")
    group = lax.axis_index("scal")
    slots, comps, depth, width = hist.shape
    steps = vel.shape[0]
    rows = field.shape[1]
    ring = rows + 8
    last = n_space - 1

    barrier = pltpu.get_barrier_semaphore()
    halo[...] = jnp.zeros_like(halo)
    for o in range(1, n_scal):
        pl.semaphore_signal(
            barrier, inc=1, device_id=(tile, lax.rem(group + o, n_scal)), device_id_type=MESH
        )
    for o in range(1, n_space):
        pl.semaphore_signal(
            barrier, inc=1, device_id=(lax.rem(tile + o, n_space), group), device_id_type=MESH
        )

    for t in range(steps):
        wanted = jnp.full((comps * depth, width), snap[t], jnp.int32)
        kept = jnp.zeros((comps * depth, width), jnp.float32)
        for k in range(slots):
            rows_k = hist[k].reshape(comps * depth, width).astype(jnp.float32)
            kept = jnp.where(wanted == group * slots + k, rows_k, kept)
        mine[t] = kept.astype(mine.dtype)

    pl.semaphore_wait(barrier, n_scal - 1 + n_space - 1)

    part_copies = []
    for o in range(1, n_scal):
        copy = pltpu.make_async_remote_copy(
            src_ref=mine, dst_ref=part.at[o], send_sem=part_send.at[o], recv_sem=part_recv.at[o],
            device_id=(tile, lax.rem(group + o, n_scal)), device_id_type=MESH,
        )
        copy.start()
        part_copies.append(copy)

    above = pltpu.make_async_remote_copy(
        src_ref=field.at[:, pl.ds(rows - 2, 2), :], dst_ref=halo.at[:, pl.ds(6, 2), :],
        send_sem=halo_send.at[0], recv_sem=halo_recv.at[0],
        device_id=(lax.rem(tile + 1, n_space), group), device_id_type=MESH,
    )
    below = pltpu.make_async_remote_copy(
        src_ref=field.at[:, pl.ds(0, 2), :], dst_ref=halo.at[:, pl.ds(0, 2), :],
        send_sem=halo_send.at[1], recv_sem=halo_recv.at[1],
        device_id=(lax.rem(tile + last, n_space), group), device_id_type=MESH,
    )

    @pl.when(tile < last)
    def _():
        above.start()

    @pl.when(tile > 0)
    def _():
        below.start()

    def window(ref):
        whole = jnp.broadcast_to(ref[...], (8, ref.shape[1]))
        total = whole.shape[1]
        turned = pltpu.roll(whole, lax.rem(total - tile * rows, total), 1)
        lane = lax.broadcasted_iota(jnp.int32, (8, LANES), 1)
        tail = pltpu.roll(turned[:, total - LANES :], ring % LANES, 1)
        return jnp.where(lane == ring - 1, tail, turned[:, :LANES])[:1]

    source, weight = window(src), window(wgt)
    index = lax.broadcasted_iota(jnp.int32, (n_space * comps * depth, LANES), 0)
    row = index // (comps * depth) * depth + index % depth
    comp = index // depth % comps
    value = jnp.where(row == source, 0.5 * (1.0 - weight), 0.0) + jnp.where(
        row == source + 1, 0.5 * weight, 0.0
    )
    first = value.astype(jnp.bfloat16).astype(jnp.float32)
    second = (value - first).astype(jnp.bfloat16).astype(jnp.float32)
    third = value - first - second
    for c in range(comps):
        for k, term in enumerate((first, second, third)):
            chosen = jnp.where(comp == c, term, 0.0).T
            select[pl.ds((c * 3 + k) * LANES, LANES), :] = chosen.astype(select.dtype)

    for copy in part_copies:
        copy.wait_recv()
    total = mine[...].astype(jnp.float32)
    for o in range(1, n_scal):
        total = total + part[o].astype(jnp.float32)
    own = pl.ds(pl.multiple_of(tile * (comps * depth), comps * depth), comps * depth)
    coarse[:, own, :] = total.astype(coarse.dtype)
    row_copies = []
    for o in range(1, n_space):
        copy = pltpu.make_async_remote_copy(
            src_ref=coarse.at[:, own, :], dst_ref=coarse.at[:, own, :],
            send_sem=row_send.at[o], recv_sem=row_recv.at[o],
            device_id=(lax.rem(tile + o, n_space), group), device_id_type=MESH,
        )
        copy.start()
        row_copies.append(copy)
    for copy in part_copies:
        copy.wait_send()
    for copy in row_copies:
        copy.wait_recv()
    for t in range(steps):
        fine = jnp.dot(select[...], coarse[t], preferred_element_type=jnp.float32)
        for c in range(comps):
            at = [(c * 3 + k) * LANES for k in range(3)]
            vel[t, c] = (fine[at[2] : at[2] + ring] + fine[at[1] : at[1] + ring]) + fine[at[0] : at[0] + ring]
    for copy in row_copies:
        copy.wait_send()

    @pl.when(tile < last)
    def _():
        above.wait_send()
        below.wait_recv()

    @pl.when(tile > 0)
    def _():
        below.wait_send()
        above.wait_recv()


def stencil_kernel(n_space, sch, halo, vel, field, out, held, made, in_sem, out_sem):
    tile = lax.axis_index("space")
    count, rows, width = field.shape
    steps = vel.shape[0]
    each = count // GROUPS
    tiles = rows // 8
    loads = []
    for g in range(GROUPS):
        part = pl.ds(g * each, each)
        loads.append(pltpu.make_async_copy(field.at[part], held.at[part], in_sem.at[g]))
        loads[-1].start()
    sub = lax.broadcasted_iota(jnp.int32, (8, width), 0)
    is_first, is_last = sub == 0, sub == 7
    outside = (is_first & (tile == n_space - 1)) | (is_last & (tile == 0))

    def advance(cells, t, diff, keep, wanted):
        ups = [pltpu.roll(u, 7, 0) for u in cells]
        downs = [pltpu.roll(u, 1, 0) for u in cells]
        n = len(cells)
        result = []
        for j in range(wanted):
            u = cells[j]
            up = jnp.where(is_last, ups[(j + 1) % n], ups[j])
            down = jnp.where(is_first, downs[(j - 1) % n], downs[j])
            east = pltpu.roll(u, width - 1, 1)
            west = pltpu.roll(u, 1, 1)
            at = pl.ds(8 * j, 8)
            result.append(
                keep * u
                + diff * ((up + down) + (east + west))
                - vel[t, 0, at, :] * (up - down)
                - vel[t, 1, at, :] * (east - west)
            )
        return result

    stores = []
    for g in range(GROUPS):
        loads[g].wait()

        def one(i, carry):
            s = g * each + i
            diff = 0.24 / jnp.full((8, LANES), sch[s], jnp.float32)
            diff = jnp.concatenate([diff] * (width // LANES), axis=1)
            keep = 1.0 - 4.0 * diff
            cells = [held[s, pl.ds(8 * j, 8), :] for j in range(tiles)] + [halo[s]]
            for t in range(steps):
                final = t == steps - 1
                cells = advance(cells, t, diff, keep, tiles if final else tiles + 1)
                if not final:
                    cells[-1] = jnp.where(outside, 0.0, cells[-1])
            for j in range(tiles):
                made[s, pl.ds(8 * j, 8), :] = cells[j]
            return carry

        lax.fori_loop(0, each, one, 0)
        part = pl.ds(g * each, each)
        stores.append(pltpu.make_async_copy(made.at[part], out.at[part], out_sem.at[g]))
        stores[-1].start()
    for store in stores:
        store.wait()


def solution(mesh):
    n_space, n_scal = mesh.shape["space"], mesh.shape["scal"]

    def body(scalars, schmidt, velocity_history, fine_src, remap_weight, snap_step):
        count, rows, width = scalars.shape
        _, comps, depth, _ = velocity_history.shape
        steps = snap_step.shape[0]
        vmem = pl.BlockSpec(memory_space=pltpu.VMEM)
        smem = pl.BlockSpec(memory_space=pltpu.SMEM)
        anywhere = pl.BlockSpec(memory_space=pl.ANY)
        own = comps * depth
        halo, vel = pl.pallas_call(
            functools.partial(gather_kernel, n_space, n_scal),
            out_shape=(
                jax.ShapeDtypeStruct((count, 8, width), jnp.float32),
                jax.ShapeDtypeStruct((steps, comps, rows + 8, width), jnp.float32),
            ),
            in_specs=[smem, vmem, vmem, vmem, anywhere],
            out_specs=(vmem, vmem),
            scratch_shapes=[
                pltpu.VMEM((steps, own, width), jnp.bfloat16),
                pltpu.VMEM((n_scal, steps, own, width), jnp.bfloat16),
                pltpu.VMEM((steps, n_space * own, width), jnp.bfloat16),
                pltpu.VMEM((3 * comps * LANES, n_space * own), jnp.bfloat16),
                pltpu.SemaphoreType.DMA((2,)),
                pltpu.SemaphoreType.DMA((2,)),
                pltpu.SemaphoreType.DMA((n_scal,)),
                pltpu.SemaphoreType.DMA((n_scal,)),
                pltpu.SemaphoreType.DMA((n_space,)),
                pltpu.SemaphoreType.DMA((n_space,)),
            ],
            compiler_params=pltpu.CompilerParams(
                collective_id=0, has_side_effects=True, vmem_limit_bytes=16 * 2**20
            ),
        )(snap_step, fine_src[None], remap_weight[None], velocity_history, scalars)
        return pl.pallas_call(
            functools.partial(stencil_kernel, n_space),
            out_shape=jax.ShapeDtypeStruct(scalars.shape, jnp.float32),
            in_specs=[smem, vmem, vmem, anywhere],
            out_specs=anywhere,
            scratch_shapes=[
                pltpu.VMEM(scalars.shape, jnp.float32),
                pltpu.VMEM(scalars.shape, jnp.float32),
                pltpu.SemaphoreType.DMA((GROUPS,)),
                pltpu.SemaphoreType.DMA((GROUPS,)),
            ],
            compiler_params=pltpu.CompilerParams(vmem_limit_bytes=24 * 2**20),
        )(schmidt, halo, vel, scalars)

    return jax.shard_map(
        body,
        mesh=mesh,
        in_specs=(
            P("scal", "space", None),
            P("scal"),
            P("scal", None, "space", None),
            P(),
            P(),
            P(),
        ),
        out_specs=P("scal", "space", None),
        check_vma=False,
    )
```

```python
import functools

import jax
import jax.numpy as jnp
from jax import lax
from jax.experimental import pallas as pl
from jax.experimental.pallas import tpu as pltpu
from jax.sharding import PartitionSpec as P

MESH = pl.DeviceIdType.MESH
LANES = 128
GROUPS = 4
TOGETHER = 2
VMEM_BYTES = 64 * 2**20


def gather_kernel(
    n_space, n_scal, snap_hbm, src_hbm, wgt_hbm, hist_hbm, field, halo, vel,
    snap, src, wgt, hist, mine, part, coarse, select, in_sem,
    halo_send, halo_recv, part_send, part_recv, row_send, row_recv,
):
    tile = lax.axis_index("space")
    group = lax.axis_index("scal")
    fetches = []
    for k, (there, here) in enumerate(
        ((snap_hbm, snap), (hist_hbm, hist), (src_hbm, src), (wgt_hbm, wgt))
    ):
        fetches.append(pltpu.make_async_copy(there, here, in_sem.at[k]))
        fetches[-1].start()
    slots, comps, depth, width = hist.shape
    halves = width // LANES
    steps = vel.shape[0]
    rows = field.shape[1]
    ring = rows + 8
    last = n_space - 1

    barrier = pltpu.get_barrier_semaphore()
    for o in range(1, n_scal):
        pl.semaphore_signal(
            barrier, inc=1, device_id=(tile, lax.rem(group + o, n_scal)), device_id_type=MESH
        )
    for o in range(1, n_space):
        pl.semaphore_signal(
            barrier, inc=1, device_id=(lax.rem(tile + o, n_space), group), device_id_type=MESH
        )

    for fetch in fetches:
        fetch.wait()

    for t in range(steps):
        wanted = jnp.full((comps * depth, width), snap[t], jnp.int32)
        kept = jnp.zeros((comps * depth, width), jnp.float32)
        for k in range(slots):
            rows_k = hist[k].reshape(comps * depth, width).astype(jnp.float32)
            kept = jnp.where(wanted == group * slots + k, rows_k, kept)
        mine[t] = kept.astype(mine.dtype)

    pl.semaphore_wait(barrier, n_scal - 1 + n_space - 1)

    part_copies = []
    for o in range(1, n_scal):
        copy = pltpu.make_async_remote_copy(
            src_ref=mine, dst_ref=part.at[o], send_sem=part_send.at[o], recv_sem=part_recv.at[o],
            device_id=(tile, lax.rem(group + o, n_scal)), device_id_type=MESH,
        )
        copy.start()
        part_copies.append(copy)

    above = pltpu.make_async_remote_copy(
        src_ref=field.at[:, pl.ds(rows - 2, 2), :], dst_ref=halo.at[:, pl.ds(6, 2), :],
        send_sem=halo_send.at[0], recv_sem=halo_recv.at[0],
        device_id=(lax.rem(tile + 1, n_space), group), device_id_type=MESH,
    )
    below = pltpu.make_async_remote_copy(
        src_ref=field.at[:, pl.ds(0, 2), :], dst_ref=halo.at[:, pl.ds(0, 2), :],
        send_sem=halo_send.at[1], recv_sem=halo_recv.at[1],
        device_id=(lax.rem(tile + last, n_space), group), device_id_type=MESH,
    )

    @pl.when(tile < last)
    def _():
        above.start()

    @pl.when(tile > 0)
    def _():
        below.start()

    def window(ref):
        whole = jnp.broadcast_to(ref[...], (8, ref.shape[1]))
        total = whole.shape[1]
        return pltpu.roll(whole, lax.rem(total + 1 - tile * rows, total), 1)[:1, :LANES]

    source, weight = window(src), window(wgt)
    index = lax.broadcasted_iota(jnp.int32, (n_space * comps * depth, LANES), 0)
    row = index // (comps * depth) * depth + index % depth
    comp = index // depth % comps
    value = jnp.where(row == source, 0.5 * (1.0 - weight), 0.0) + jnp.where(
        row == source + 1, 0.5 * weight, 0.0
    )
    first = value.astype(jnp.bfloat16).astype(jnp.float32)
    second = (value - first).astype(jnp.bfloat16).astype(jnp.float32)
    third = value - first - second
    for c in range(comps):
        for k, term in enumerate((first, second, third)):
            chosen = jnp.where(comp == c, term, 0.0).T
            select[pl.ds((c * 3 + k) * LANES, LANES), :] = chosen.astype(select.dtype)

    for copy in part_copies:
        copy.wait_recv()
    total = mine[...].astype(jnp.float32)
    for o in range(1, n_scal):
        total = total + part[o].astype(jnp.float32)
    own = pl.ds(pl.multiple_of(tile * (comps * depth), comps * depth), comps * depth)
    coarse[:, own, :] = total.astype(coarse.dtype)
    row_copies = []
    for o in range(1, n_space):
        copy = pltpu.make_async_remote_copy(
            src_ref=coarse.at[:, own, :], dst_ref=coarse.at[:, own, :],
            send_sem=row_send.at[o], recv_sem=row_recv.at[o],
            device_id=(lax.rem(tile + o, n_space), group), device_id_type=MESH,
        )
        copy.start()
        row_copies.append(copy)
    for copy in part_copies:
        copy.wait_send()
    for copy in row_copies:
        copy.wait_recv()
    for t in range(steps):
        fine = jnp.dot(select[...], coarse[t], preferred_element_type=jnp.float32)
        for c in range(comps):
            at = [(c * 3 + k) * LANES for k in range(3)]
            both = (fine[at[2] : at[2] + ring] + fine[at[1] : at[1] + ring]) + fine[at[0] : at[0] + ring]
            for h in range(halves):
                vel[t, c, h] = both[:, h * LANES : (h + 1) * LANES]
    for copy in row_copies:
        copy.wait_send()

    @pl.when(tile < last)
    def _():
        above.wait_send()
        below.wait_recv()

    @pl.when(tile > 0)
    def _():
        below.wait_send()
        above.wait_recv()


def stencil_kernel(
    n_space, sch_hbm, halo, vel_hbm, field, out,
    sch, vel, held, step, made, few_sem, in_sem, out_sem,
):
    tile = lax.axis_index("space")
    count, rows, width = field.shape
    halves = width // LANES
    each = count // GROUPS
    few = [
        pltpu.make_async_copy(sch_hbm, sch, few_sem.at[0]),
        pltpu.make_async_copy(vel_hbm, vel, few_sem.at[1]),
    ]
    for copy in few:
        copy.start()
    loads = []
    for g in range(GROUPS):
        part = pl.ds(g * each, each)
        loads.append([])
        for h in range(halves):
            lanes = pl.ds(h * LANES, LANES)
            for k, (there, at, long) in enumerate(
                ((field, 8, rows), (halo, 0, 8), (halo, rows + 8, 8))
            ):
                loads[-1].append(pltpu.make_async_copy(
                    there.at[part, :, lanes], held.at[part, h, pl.ds(at, long), :], in_sem.at[g, h, k]
                ))
                loads[-1][-1].start()
    sub = lax.broadcasted_iota(jnp.int32, (8, LANES), 0)
    lane = lax.broadcasted_iota(jnp.int32, (8, LANES), 1)
    top = (sub == 0) & (tile == 0)
    bottom = (sub == 1) & (tile == n_space - 1)

    def advance(t, source, at, row, diffs):
        v0 = [vel[t, 0, h, pl.ds(row, 8), :] for h in range(halves)]
        v1 = [vel[t, 1, h, pl.ds(row, 8), :] for h in range(halves)]
        result = []
        for k, (diff, keep) in enumerate(diffs):
            u = [source(k, h, at) for h in range(halves)]
            easts = [pltpu.roll(x, LANES - 1, 1) for x in u]
            wests = [pltpu.roll(x, 1, 1) for x in u]
            for h in range(halves):
                up, down = source(k, h, at + 1), source(k, h, at - 1)
                east = jnp.where(lane == LANES - 1, easts[(h + 1) % halves], easts[h])
                west = jnp.where(lane == 0, wests[(h - 1) % halves], wests[h])
                result.append(
                    keep * u[h]
                    + diff * ((up + down) + (east + west))
                    - v0[h] * (up - down)
                    - v1[h] * (east - west)
                )
        return result

    stores = []
    for g in range(GROUPS):
        for load in loads[g]:
            load.wait()
        if g == 0:
            for copy in few:
                copy.wait()

        @pl.when(tile == 0)
        def _():
            held[pl.ds(g * each, each), :, pl.ds(0, 8), :] = jnp.zeros((each, halves, 8, LANES), jnp.float32)

        @pl.when(tile == n_space - 1)
        def _():
            held[pl.ds(g * each, each), :, pl.ds(rows + 8, 8), :] = jnp.zeros((each, halves, 8, LANES), jnp.float32)

        def some(i, carry):
            base = g * each + i * TOGETHER
            diffs = []
            for k in range(TOGETHER):
                diff = 0.24 / jnp.full((8, LANES), sch[base + k], jnp.float32)
                diffs.append((diff, 1.0 - 4.0 * diff))

            def before(k, h, at):
                return held[base + k, h, pl.ds(at, 8), :]

            def after(k, h, at):
                return step[k, h, pl.ds(at, 8), :]

            for j in range(rows // 8 + 1):
                at = 8 * j + 7
                for n, value in enumerate(advance(0, before, at, 8 * j, diffs)):
                    if j == 0:
                        value = jnp.where(top, 0.0, value)
                    if j == rows // 8:
                        value = jnp.where(bottom, 0.0, value)
                    step[n // halves, n % halves, pl.ds(at, 8), :] = value
            for j in range(rows // 8):
                for n, value in enumerate(advance(1, after, 8 * j + 8, 8 * j + 1, diffs)):
                    made[base + n // halves, n % halves, pl.ds(8 * j, 8), :] = value
            return carry

        lax.fori_loop(0, each // TOGETHER, some, 0)
        part = pl.ds(g * each, each)
        for h in range(halves):
            stores.append(pltpu.make_async_copy(
                made.at[part, h], out.at[part, :, pl.ds(h * LANES, LANES)], out_sem.at[g, h]
            ))
            stores[-1].start()
    for store in stores:
        store.wait()


def solution(mesh):
    n_space, n_scal = mesh.shape["space"], mesh.shape["scal"]

    def body(scalars, schmidt, velocity_history, fine_src, remap_weight, snap_step):
        count, rows, width = scalars.shape
        _, comps, depth, _ = velocity_history.shape
        steps = snap_step.shape[0]
        vmem = pl.BlockSpec(memory_space=pltpu.VMEM)
        hbm = pl.BlockSpec(memory_space=pltpu.HBM)
        halves = width // LANES
        own = comps * depth
        halo, vel = pl.pallas_call(
            functools.partial(gather_kernel, n_space, n_scal),
            out_shape=(
                jax.ShapeDtypeStruct((count, 8, width), jnp.float32),
                jax.ShapeDtypeStruct((steps, comps, halves, rows + 8, LANES), jnp.float32),
            ),
            in_specs=[hbm] * 5,
            out_specs=(hbm, vmem),
            scratch_shapes=[
                pltpu.SMEM(snap_step.shape, jnp.int32),
                pltpu.VMEM((1,) + fine_src.shape, jnp.int32),
                pltpu.VMEM((1,) + remap_weight.shape, jnp.float32),
                pltpu.VMEM(velocity_history.shape, velocity_history.dtype),
                pltpu.VMEM((steps, own, width), jnp.bfloat16),
                pltpu.VMEM((n_scal, steps, own, width), jnp.bfloat16),
                pltpu.VMEM((steps, n_space * own, width), jnp.bfloat16),
                pltpu.VMEM((3 * comps * LANES, n_space * own), jnp.bfloat16),
                pltpu.SemaphoreType.DMA((4,)),
                pltpu.SemaphoreType.DMA((2,)),
                pltpu.SemaphoreType.DMA((2,)),
                pltpu.SemaphoreType.DMA((n_scal,)),
                pltpu.SemaphoreType.DMA((n_scal,)),
                pltpu.SemaphoreType.DMA((n_space,)),
                pltpu.SemaphoreType.DMA((n_space,)),
            ],
            compiler_params=pltpu.CompilerParams(
                collective_id=0, has_side_effects=True, vmem_limit_bytes=VMEM_BYTES
            ),
        )(snap_step, fine_src[None], remap_weight[None], velocity_history, scalars)
        return pl.pallas_call(
            functools.partial(stencil_kernel, n_space),
            out_shape=jax.ShapeDtypeStruct(scalars.shape, jnp.float32),
            in_specs=[hbm] * 4,
            out_specs=hbm,
            scratch_shapes=[
                pltpu.SMEM(schmidt.shape, jnp.float32),
                pltpu.VMEM((steps, comps, halves, rows + 8, LANES), jnp.float32),
                pltpu.VMEM((count, halves, rows + 16, LANES), jnp.float32),
                pltpu.VMEM((TOGETHER, halves, rows + 16, LANES), jnp.float32),
                pltpu.VMEM((count, halves, rows, LANES), jnp.float32),
                pltpu.SemaphoreType.DMA((2,)),
                pltpu.SemaphoreType.DMA((GROUPS, halves, 3)),
                pltpu.SemaphoreType.DMA((GROUPS, halves)),
            ],
            compiler_params=pltpu.CompilerParams(vmem_limit_bytes=VMEM_BYTES),
        )(schmidt, halo, vel, scalars)

    return jax.shard_map(
        body,
        mesh=mesh,
        in_specs=(
            P("scal", "space", None),
            P("scal"),
            P("scal", None, "space", None),
            P(),
            P(),
            P(),
        ),
        out_specs=P("scal", "space", None),
        check_vma=False,
    )
```

```python
import functools

import jax
import jax.numpy as jnp
from jax import lax
from jax.experimental import pallas as pl
from jax.experimental.pallas import tpu as pltpu
from jax.sharding import PartitionSpec as P

MESH = pl.DeviceIdType.MESH
LANES = 128
GROUPS = 4
TOGETHER = 8
VMEM_BYTES = 64 * 2**20


def gather_kernel(
    n_space, n_scal, snap_hbm, src_hbm, wgt_hbm, hist_hbm, field, halo, vel,
    snap, src, wgt, hist, mine, part, coarse, select, in_sem,
    halo_send, halo_recv, part_send, part_recv, row_send, row_recv,
):
    tile = lax.axis_index("space")
    group = lax.axis_index("scal")
    fetches = []
    for k, (there, here) in enumerate(
        ((snap_hbm, snap), (hist_hbm, hist), (src_hbm, src), (wgt_hbm, wgt))
    ):
        fetches.append(pltpu.make_async_copy(there, here, in_sem.at[k]))
        fetches[-1].start()
    slots, comps, depth, width = hist.shape
    halves = width // LANES
    steps = vel.shape[0]
    rows = field.shape[1]
    ring = rows + 8
    last = n_space - 1

    barrier = pltpu.get_barrier_semaphore()
    for o in range(1, n_scal):
        pl.semaphore_signal(
            barrier, inc=1, device_id=(tile, lax.rem(group + o, n_scal)), device_id_type=MESH
        )
    for o in range(1, n_space):
        pl.semaphore_signal(
            barrier, inc=1, device_id=(lax.rem(tile + o, n_space), group), device_id_type=MESH
        )

    for fetch in fetches:
        fetch.wait()

    for t in range(steps):
        wanted = jnp.full((comps * depth, width), snap[t], jnp.int32)
        kept = jnp.zeros((comps * depth, width), jnp.float32)
        for k in range(slots):
            rows_k = hist[k].reshape(comps * depth, width).astype(jnp.float32)
            kept = jnp.where(wanted == group * slots + k, rows_k, kept)
        mine[t] = kept.astype(mine.dtype)

    pl.semaphore_wait(barrier, n_scal - 1 + n_space - 1)

    part_copies = []
    for o in range(1, n_scal):
        copy = pltpu.make_async_remote_copy(
            src_ref=mine, dst_ref=part.at[o], send_sem=part_send.at[o], recv_sem=part_recv.at[o],
            device_id=(tile, lax.rem(group + o, n_scal)), device_id_type=MESH,
        )
        copy.start()
        part_copies.append(copy)

    above = pltpu.make_async_remote_copy(
        src_ref=field.at[:, pl.ds(rows - 2, 2), :], dst_ref=halo.at[:, pl.ds(6, 2), :],
        send_sem=halo_send.at[0], recv_sem=halo_recv.at[0],
        device_id=(lax.rem(tile + 1, n_space), group), device_id_type=MESH,
    )
    below = pltpu.make_async_remote_copy(
        src_ref=field.at[:, pl.ds(0, 2), :], dst_ref=halo.at[:, pl.ds(0, 2), :],
        send_sem=halo_send.at[1], recv_sem=halo_recv.at[1],
        device_id=(lax.rem(tile + last, n_space), group), device_id_type=MESH,
    )

    @pl.when(tile < last)
    def _():
        above.start()

    @pl.when(tile > 0)
    def _():
        below.start()

    def window(ref):
        whole = jnp.broadcast_to(ref[...], (8, ref.shape[1]))
        total = whole.shape[1]
        return pltpu.roll(whole, lax.rem(total + 1 - tile * rows, total), 1)[:1, :LANES]

    source, weight = window(src), window(wgt)
    index = lax.broadcasted_iota(jnp.int32, (n_space * comps * depth, LANES), 0)
    row = index // (comps * depth) * depth + index % depth
    comp = index // depth % comps
    value = jnp.where(row == source, 0.5 * (1.0 - weight), 0.0) + jnp.where(
        row == source + 1, 0.5 * weight, 0.0
    )
    first = value.astype(jnp.bfloat16).astype(jnp.float32)
    second = (value - first).astype(jnp.bfloat16).astype(jnp.float32)
    third = value - first - second
    for c in range(comps):
        for k, term in enumerate((first, second, third)):
            chosen = jnp.where(comp == c, term, 0.0).T
            select[pl.ds((c * 3 + k) * LANES, LANES), :] = chosen.astype(select.dtype)

    for copy in part_copies:
        copy.wait_recv()
    total = mine[...].astype(jnp.float32)
    for o in range(1, n_scal):
        total = total + part[o].astype(jnp.float32)
    own = pl.ds(pl.multiple_of(tile * (comps * depth), comps * depth), comps * depth)
    coarse[:, own, :] = total.astype(coarse.dtype)
    row_copies = []
    for o in range(1, n_space):
        copy = pltpu.make_async_remote_copy(
            src_ref=coarse.at[:, own, :], dst_ref=coarse.at[:, own, :],
            send_sem=row_send.at[o], recv_sem=row_recv.at[o],
            device_id=(lax.rem(tile + o, n_space), group), device_id_type=MESH,
        )
        copy.start()
        row_copies.append(copy)
    for copy in part_copies:
        copy.wait_send()
    for copy in row_copies:
        copy.wait_recv()
    for t in range(steps):
        fine = jnp.dot(select[...], coarse[t], preferred_element_type=jnp.float32)
        for c in range(comps):
            at = [(c * 3 + k) * LANES for k in range(3)]
            both = (fine[at[2] : at[2] + ring] + fine[at[1] : at[1] + ring]) + fine[at[0] : at[0] + ring]
            for h in range(halves):
                vel[t, c, h] = both[:, h * LANES : (h + 1) * LANES]
    for copy in row_copies:
        copy.wait_send()

    @pl.when(tile < last)
    def _():
        above.wait_send()
        below.wait_recv()

    @pl.when(tile > 0)
    def _():
        below.wait_send()
        above.wait_recv()


def stencil_kernel(
    n_space, sch_hbm, halo, vel_hbm, field, out,
    sch, vel, held, step, made, few_sem, in_sem, out_sem,
):
    tile = lax.axis_index("space")
    count, rows, width = field.shape
    halves = width // LANES
    each = count // GROUPS
    few = [
        pltpu.make_async_copy(sch_hbm, sch, few_sem.at[0]),
        pltpu.make_async_copy(vel_hbm, vel, few_sem.at[1]),
    ]
    for copy in few:
        copy.start()
    loads = []
    for g in range(GROUPS):
        part = pl.ds(g * each, each)
        loads.append([])
        for h in range(halves):
            lanes = pl.ds(h * LANES, LANES)
            for k, (there, at, long) in enumerate(
                ((field, 8, rows), (halo, 0, 8), (halo, rows + 8, 8))
            ):
                loads[-1].append(pltpu.make_async_copy(
                    there.at[part, :, lanes], held.at[part, h, pl.ds(at, long), :], in_sem.at[g, h, k]
                ))
                loads[-1][-1].start()
    sub = lax.broadcasted_iota(jnp.int32, (8, LANES), 0)
    lane = lax.broadcasted_iota(jnp.int32, (8, LANES), 1)
    top = (sub == 0) & (tile == 0)
    bottom = (sub == 1) & (tile == n_space - 1)

    def advance(t, source, at, row, diffs):
        v0 = [vel[t, 0, h, pl.ds(row, 8), :] for h in range(halves)]
        v1 = [vel[t, 1, h, pl.ds(row, 8), :] for h in range(halves)]
        result = []
        for k, (diff, keep) in enumerate(diffs):
            u = [source(k, h, at) for h in range(halves)]
            easts = [pltpu.roll(x, LANES - 1, 1) for x in u]
            wests = [pltpu.roll(x, 1, 1) for x in u]
            for h in range(halves):
                up, down = source(k, h, at + 1), source(k, h, at - 1)
                east = jnp.where(lane == LANES - 1, easts[(h + 1) % halves], easts[h])
                west = jnp.where(lane == 0, wests[(h - 1) % halves], wests[h])
                result.append(
                    keep * u[h]
                    + diff * ((up + down) + (east + west))
                    - v0[h] * (up - down)
                    - v1[h] * (east - west)
                )
        return result

    stores = []
    for g in range(GROUPS):
        for load in loads[g]:
            load.wait()
        if g == 0:
            for copy in few:
                copy.wait()

        @pl.when(tile == 0)
        def _():
            held[pl.ds(g * each, each), :, pl.ds(0, 8), :] = jnp.zeros((each, halves, 8, LANES), jnp.float32)

        @pl.when(tile == n_space - 1)
        def _():
            held[pl.ds(g * each, each), :, pl.ds(rows + 8, 8), :] = jnp.zeros((each, halves, 8, LANES), jnp.float32)

        def some(i, carry):
            base = g * each + i * TOGETHER
            diffs = []
            for k in range(TOGETHER):
                diff = 0.24 / jnp.full((8, LANES), sch[base + k], jnp.float32)
                diffs.append((diff, 1.0 - 4.0 * diff))

            def before(k, h, at):
                return held[base + k, h, pl.ds(at, 8), :]

            def after(k, h, at):
                return step[k, h, pl.ds(at, 8), :]

            for j in range(rows // 8 + 1):
                at = 8 * j + 7
                for n, value in enumerate(advance(0, before, at, 8 * j, diffs)):
                    if j == 0:
                        value = jnp.where(top, 0.0, value)
                    if j == rows // 8:
                        value = jnp.where(bottom, 0.0, value)
                    step[n // halves, n % halves, pl.ds(at, 8), :] = value
            for j in range(rows // 8):
                for n, value in enumerate(advance(1, after, 8 * j + 8, 8 * j + 1, diffs)):
                    made[base + n // halves, n % halves, pl.ds(8 * j, 8), :] = value
            return carry

        lax.fori_loop(0, each // TOGETHER, some, 0)
        part = pl.ds(g * each, each)
        for h in range(halves):
            stores.append(pltpu.make_async_copy(
                made.at[part, h], out.at[part, :, pl.ds(h * LANES, LANES)], out_sem.at[g, h]
            ))
            stores[-1].start()
    for store in stores:
        store.wait()


def solution(mesh):
    n_space, n_scal = mesh.shape["space"], mesh.shape["scal"]

    def body(scalars, schmidt, velocity_history, fine_src, remap_weight, snap_step):
        count, rows, width = scalars.shape
        _, comps, depth, _ = velocity_history.shape
        steps = snap_step.shape[0]
        vmem = pl.BlockSpec(memory_space=pltpu.VMEM)
        hbm = pl.BlockSpec(memory_space=pltpu.HBM)
        halves = width // LANES
        own = comps * depth
        halo, vel = pl.pallas_call(
            functools.partial(gather_kernel, n_space, n_scal),
            out_shape=(
                jax.ShapeDtypeStruct((count, 8, width), jnp.float32),
                jax.ShapeDtypeStruct((steps, comps, halves, rows + 8, LANES), jnp.float32),
            ),
            in_specs=[hbm] * 5,
            out_specs=(hbm, vmem),
            scratch_shapes=[
                pltpu.SMEM(snap_step.shape, jnp.int32),
                pltpu.VMEM((1,) + fine_src.shape, jnp.int32),
                pltpu.VMEM((1,) + remap_weight.shape, jnp.float32),
                pltpu.VMEM(velocity_history.shape, velocity_history.dtype),
                pltpu.VMEM((steps, own, width), jnp.bfloat16),
                pltpu.VMEM((n_scal, steps, own, width), jnp.bfloat16),
                pltpu.VMEM((steps, n_space * own, width), jnp.bfloat16),
                pltpu.VMEM((3 * comps * LANES, n_space * own), jnp.bfloat16),
                pltpu.SemaphoreType.DMA((4,)),
                pltpu.SemaphoreType.DMA((2,)),
                pltpu.SemaphoreType.DMA((2,)),
                pltpu.SemaphoreType.DMA((n_scal,)),
                pltpu.SemaphoreType.DMA((n_scal,)),
                pltpu.SemaphoreType.DMA((n_space,)),
                pltpu.SemaphoreType.DMA((n_space,)),
            ],
            compiler_params=pltpu.CompilerParams(
                collective_id=0, has_side_effects=True, vmem_limit_bytes=VMEM_BYTES
            ),
        )(snap_step, fine_src[None], remap_weight[None], velocity_history, scalars)
        return pl.pallas_call(
            functools.partial(stencil_kernel, n_space),
            out_shape=jax.ShapeDtypeStruct(scalars.shape, jnp.float32),
            in_specs=[hbm] * 4,
            out_specs=hbm,
            scratch_shapes=[
                pltpu.SMEM(schmidt.shape, jnp.float32),
                pltpu.VMEM((steps, comps, halves, rows + 8, LANES), jnp.float32),
                pltpu.VMEM((count, halves, rows + 16, LANES), jnp.float32),
                pltpu.VMEM((TOGETHER, halves, rows + 16, LANES), jnp.float32),
                pltpu.VMEM((count, halves, rows, LANES), jnp.float32),
                pltpu.SemaphoreType.DMA((2,)),
                pltpu.SemaphoreType.DMA((GROUPS, halves, 3)),
                pltpu.SemaphoreType.DMA((GROUPS, halves)),
            ],
            compiler_params=pltpu.CompilerParams(vmem_limit_bytes=VMEM_BYTES),
        )(schmidt, halo, vel, scalars)

    return jax.shard_map(
        body,
        mesh=mesh,
        in_specs=(
            P("scal", "space", None),
            P("scal"),
            P("scal", None, "space", None),
            P(),
            P(),
            P(),
        ),
        out_specs=P("scal", "space", None),
        check_vma=False,
    )
```

```python
import functools

import jax
import jax.numpy as jnp
from jax import lax
from jax.experimental import pallas as pl
from jax.experimental.pallas import tpu as pltpu
from jax.sharding import PartitionSpec as P

MESH = pl.DeviceIdType.MESH
LANES = 128
GROUPS = 4
TOGETHER = 8
VMEM_BYTES = 64 * 2**20


def gather_kernel(
    n_space, n_scal, snap_hbm, src_hbm, wgt_hbm, hist_hbm, field, halo, vel,
    snap, src, wgt, hist, mine, part, coarse, select, in_sem,
    halo_send, halo_recv, part_send, part_recv, row_send, row_recv,
):
    tile = lax.axis_index("space")
    group = lax.axis_index("scal")
    fetches = []
    for k, (there, here) in enumerate(
        ((snap_hbm, snap), (hist_hbm, hist), (src_hbm, src), (wgt_hbm, wgt))
    ):
        fetches.append(pltpu.make_async_copy(there, here, in_sem.at[k]))
        fetches[-1].start()
    slots, comps, depth, width = hist.shape
    halves = width // LANES
    steps = vel.shape[0]
    rows = field.shape[1]
    ring = rows + 8
    last = n_space - 1

    barrier = pltpu.get_barrier_semaphore()
    for o in range(1, n_scal):
        pl.semaphore_signal(
            barrier, inc=1, device_id=(tile, lax.rem(group + o, n_scal)), device_id_type=MESH
        )
    for o in range(1, n_space):
        pl.semaphore_signal(
            barrier, inc=1, device_id=(lax.rem(tile + o, n_space), group), device_id_type=MESH
        )

    for fetch in fetches:
        fetch.wait()

    for t in range(steps):
        wanted = jnp.full((comps * depth, width), snap[t], jnp.int32)
        kept = jnp.zeros((comps * depth, width), jnp.float32)
        for k in range(slots):
            rows_k = hist[k].reshape(comps * depth, width).astype(jnp.float32)
            kept = jnp.where(wanted == group * slots + k, rows_k, kept)
        mine[t] = kept.astype(mine.dtype)

    pl.semaphore_wait(barrier, n_scal - 1 + n_space - 1)

    part_copies = []
    for o in range(1, n_scal):
        copy = pltpu.make_async_remote_copy(
            src_ref=mine, dst_ref=part.at[o], send_sem=part_send.at[o], recv_sem=part_recv.at[o],
            device_id=(tile, lax.rem(group + o, n_scal)), device_id_type=MESH,
        )
        copy.start()
        part_copies.append(copy)

    above = pltpu.make_async_remote_copy(
        src_ref=field.at[:, pl.ds(rows - 2, 2), :], dst_ref=halo.at[:, pl.ds(6, 2), :],
        send_sem=halo_send.at[0], recv_sem=halo_recv.at[0],
        device_id=(lax.rem(tile + 1, n_space), group), device_id_type=MESH,
    )
    below = pltpu.make_async_remote_copy(
        src_ref=field.at[:, pl.ds(0, 2), :], dst_ref=halo.at[:, pl.ds(0, 2), :],
        send_sem=halo_send.at[1], recv_sem=halo_recv.at[1],
        device_id=(lax.rem(tile + last, n_space), group), device_id_type=MESH,
    )

    def window(ref):
        whole = jnp.broadcast_to(ref[...], (8, ref.shape[1]))
        total = whole.shape[1]
        return pltpu.roll(whole, lax.rem(total + 1 - tile * rows, total), 1)[:1, :LANES]

    source, weight = window(src), window(wgt)
    index = lax.broadcasted_iota(jnp.int32, (n_space * comps * depth, LANES), 0)
    row = index // (comps * depth) * depth + index % depth
    comp = index // depth % comps
    value = jnp.where(row == source, 0.5 * (1.0 - weight), 0.0) + jnp.where(
        row == source + 1, 0.5 * weight, 0.0
    )
    first = value.astype(jnp.bfloat16).astype(jnp.float32)
    second = (value - first).astype(jnp.bfloat16).astype(jnp.float32)
    third = value - first - second
    for c in range(comps):
        for k, term in enumerate((first, second, third)):
            chosen = jnp.where(comp == c, term, 0.0).T
            select[pl.ds((c * 3 + k) * LANES, LANES), :] = chosen.astype(select.dtype)

    for copy in part_copies:
        copy.wait_recv()
    total = mine[...].astype(jnp.float32)
    for o in range(1, n_scal):
        total = total + part[o].astype(jnp.float32)
    own = pl.ds(pl.multiple_of(tile * (comps * depth), comps * depth), comps * depth)
    coarse[:, own, :] = total.astype(coarse.dtype)
    row_copies = []
    for o in range(1, n_space):
        copy = pltpu.make_async_remote_copy(
            src_ref=coarse.at[:, own, :], dst_ref=coarse.at[:, own, :],
            send_sem=row_send.at[o], recv_sem=row_recv.at[o],
            device_id=(lax.rem(tile + o, n_space), group), device_id_type=MESH,
        )
        copy.start()
        row_copies.append(copy)

    @pl.when(tile < last)
    def _():
        above.start()

    @pl.when(tile > 0)
    def _():
        below.start()

    for copy in part_copies:
        copy.wait_send()
    for copy in row_copies:
        copy.wait_recv()
    for t in range(steps):
        fine = jnp.dot(select[...], coarse[t], preferred_element_type=jnp.float32)
        for c in range(comps):
            at = [(c * 3 + k) * LANES for k in range(3)]
            both = (fine[at[2] : at[2] + ring] + fine[at[1] : at[1] + ring]) + fine[at[0] : at[0] + ring]
            for h in range(halves):
                vel[t, c, h] = both[:, h * LANES : (h + 1) * LANES]
    for copy in row_copies:
        copy.wait_send()

    @pl.when(tile < last)
    def _():
        above.wait_send()
        below.wait_recv()

    @pl.when(tile > 0)
    def _():
        below.wait_send()
        above.wait_recv()


def stencil_kernel(
    n_space, sch_hbm, halo, vel_hbm, field, out,
    sch, vel, held, step, made, few_sem, in_sem, out_sem,
):
    tile = lax.axis_index("space")
    count, rows, width = field.shape
    halves = width // LANES
    each = count // GROUPS
    few = [
        pltpu.make_async_copy(sch_hbm, sch, few_sem.at[0]),
        pltpu.make_async_copy(vel_hbm, vel, few_sem.at[1]),
    ]
    for copy in few:
        copy.start()
    loads = []
    for g in range(GROUPS):
        part = pl.ds(g * each, each)
        loads.append([])
        for h in range(halves):
            lanes = pl.ds(h * LANES, LANES)
            for k, (there, at, long) in enumerate(
                ((field, 8, rows), (halo, 0, 8), (halo, rows + 8, 8))
            ):
                loads[-1].append(pltpu.make_async_copy(
                    there.at[part, :, lanes], held.at[part, h, pl.ds(at, long), :], in_sem.at[g, h, k]
                ))
                loads[-1][-1].start()
    sub = lax.broadcasted_iota(jnp.int32, (8, LANES), 0)
    lane = lax.broadcasted_iota(jnp.int32, (8, LANES), 1)
    top = (sub == 0) & (tile == 0)
    bottom = (sub == 1) & (tile == n_space - 1)

    def advance(t, source, at, row, diffs):
        v0 = [vel[t, 0, h, pl.ds(row, 8), :] for h in range(halves)]
        v1 = [vel[t, 1, h, pl.ds(row, 8), :] for h in range(halves)]
        result = []
        for k, (diff, keep) in enumerate(diffs):
            u = [source(k, h, at) for h in range(halves)]
            easts = [pltpu.roll(x, LANES - 1, 1) for x in u]
            wests = [pltpu.roll(x, 1, 1) for x in u]
            for h in range(halves):
                up, down = source(k, h, at + 1), source(k, h, at - 1)
                east = jnp.where(lane == LANES - 1, easts[(h + 1) % halves], easts[h])
                west = jnp.where(lane == 0, wests[(h - 1) % halves], wests[h])
                result.append(
                    keep * u[h]
                    + diff * ((up + down) + (east + west))
                    - v0[h] * (up - down)
                    - v1[h] * (east - west)
                )
        return result

    stores = []
    for g in range(GROUPS):
        for load in loads[g]:
            load.wait()
        if g == 0:
            for copy in few:
                copy.wait()

        @pl.when(tile == 0)
        def _():
            held[pl.ds(g * each, each), :, pl.ds(0, 8), :] = jnp.zeros((each, halves, 8, LANES), jnp.float32)

        @pl.when(tile == n_space - 1)
        def _():
            held[pl.ds(g * each, each), :, pl.ds(rows + 8, 8), :] = jnp.zeros((each, halves, 8, LANES), jnp.float32)

        def some(i, carry):
            base = g * each + i * TOGETHER
            diffs = []
            for k in range(TOGETHER):
                diff = 0.24 / jnp.full((8, LANES), sch[base + k], jnp.float32)
                diffs.append((diff, 1.0 - 4.0 * diff))

            def before(k, h, at):
                return held[base + k, h, pl.ds(at, 8), :]

            def after(k, h, at):
                return step[k, h, pl.ds(at, 8), :]

            for j in range(rows // 8 + 1):
                at = 8 * j + 7
                for n, value in enumerate(advance(0, before, at, 8 * j, diffs)):
                    if j == 0:
                        value = jnp.where(top, 0.0, value)
                    if j == rows // 8:
                        value = jnp.where(bottom, 0.0, value)
                    step[n // halves, n % halves, pl.ds(at, 8), :] = value
            for j in range(rows // 8):
                for n, value in enumerate(advance(1, after, 8 * j + 8, 8 * j + 1, diffs)):
                    made[base + n // halves, n % halves, pl.ds(8 * j, 8), :] = value
            return carry

        lax.fori_loop(0, each // TOGETHER, some, 0)
        part = pl.ds(g * each, each)
        for h in range(halves):
            stores.append(pltpu.make_async_copy(
                made.at[part, h], out.at[part, :, pl.ds(h * LANES, LANES)], out_sem.at[g, h]
            ))
            stores[-1].start()
    for store in stores:
        store.wait()


def solution(mesh):
    n_space, n_scal = mesh.shape["space"], mesh.shape["scal"]

    def body(scalars, schmidt, velocity_history, fine_src, remap_weight, snap_step):
        count, rows, width = scalars.shape
        _, comps, depth, _ = velocity_history.shape
        steps = snap_step.shape[0]
        vmem = pl.BlockSpec(memory_space=pltpu.VMEM)
        hbm = pl.BlockSpec(memory_space=pltpu.HBM)
        halves = width // LANES
        own = comps * depth
        halo, vel = pl.pallas_call(
            functools.partial(gather_kernel, n_space, n_scal),
            out_shape=(
                jax.ShapeDtypeStruct((count, 8, width), jnp.float32),
                jax.ShapeDtypeStruct((steps, comps, halves, rows + 8, LANES), jnp.float32),
            ),
            in_specs=[hbm] * 5,
            out_specs=(hbm, vmem),
            scratch_shapes=[
                pltpu.SMEM(snap_step.shape, jnp.int32),
                pltpu.VMEM((1,) + fine_src.shape, jnp.int32),
                pltpu.VMEM((1,) + remap_weight.shape, jnp.float32),
                pltpu.VMEM(velocity_history.shape, velocity_history.dtype),
                pltpu.VMEM((steps, own, width), jnp.bfloat16),
                pltpu.VMEM((n_scal, steps, own, width), jnp.bfloat16),
                pltpu.VMEM((steps, n_space * own, width), jnp.bfloat16),
                pltpu.VMEM((3 * comps * LANES, n_space * own), jnp.bfloat16),
                pltpu.SemaphoreType.DMA((4,)),
                pltpu.SemaphoreType.DMA((2,)),
                pltpu.SemaphoreType.DMA((2,)),
                pltpu.SemaphoreType.DMA((n_scal,)),
                pltpu.SemaphoreType.DMA((n_scal,)),
                pltpu.SemaphoreType.DMA((n_space,)),
                pltpu.SemaphoreType.DMA((n_space,)),
            ],
            compiler_params=pltpu.CompilerParams(
                collective_id=0, has_side_effects=True, vmem_limit_bytes=VMEM_BYTES
            ),
        )(snap_step, fine_src[None], remap_weight[None], velocity_history, scalars)
        return pl.pallas_call(
            functools.partial(stencil_kernel, n_space),
            out_shape=jax.ShapeDtypeStruct(scalars.shape, jnp.float32),
            in_specs=[hbm] * 4,
            out_specs=hbm,
            scratch_shapes=[
                pltpu.SMEM(schmidt.shape, jnp.float32),
                pltpu.VMEM((steps, comps, halves, rows + 8, LANES), jnp.float32),
                pltpu.VMEM((count, halves, rows + 16, LANES), jnp.float32),
                pltpu.VMEM((TOGETHER, halves, rows + 16, LANES), jnp.float32),
                pltpu.VMEM((count, halves, rows, LANES), jnp.float32),
                pltpu.SemaphoreType.DMA((2,)),
                pltpu.SemaphoreType.DMA((GROUPS, halves, 3)),
                pltpu.SemaphoreType.DMA((GROUPS, halves)),
            ],
            compiler_params=pltpu.CompilerParams(vmem_limit_bytes=VMEM_BYTES),
        )(schmidt, halo, vel, scalars)

    return jax.shard_map(
        body,
        mesh=mesh,
        in_specs=(
            P("scal", "space", None),
            P("scal"),
            P("scal", None, "space", None),
            P(),
            P(),
            P(),
        ),
        out_specs=P("scal", "space", None),
        check_vma=False,
    )
```
